32 devices in a mesh: cache: 8 (over y, x, core), head: 4 (over z).
Axes of the slice: x: 2, y: 2, z: 4, core: 2. Of those that a mesh axis runs over, the one named last changes fastest.
Arguments:
- tokens: bfloat16 [6144, 8192], P('cache'), may hold values from -6 to 6
- w_x: bfloat16 [8192, 8192], P('cache', 'head'), may hold values from -0.0625 to 0.0625
- w_bc: bfloat16 [8192, 8, 512], P('cache', 'head'), may hold values from -1 to 1
- w_dt: bfloat16 [8192, 128], P('cache', 'head'), may hold values from -0.0625 to 0.0625
- dt_bias: float32 [128], P('head'), may hold values from -3 to -1
- decay_log: float32 [128], P('head'), may hold values from -6.2 to -0.8
- skip_gain: float32 [128], P('head'), may hold values from 0.5 to 1.5
- pool: bfloat16 [64, 256, 8192], P('cache', 'head'), may hold values from -6 to 6
- owners: int32 [48, 1], replicated, may hold values from 0 to 7, as said below
- slots: int32 [48, 1], replicated, may hold values from 0 to 7
- offsets: int32 [48], P('cache'), may hold values from 0 to 31
Outputs:
- mixed: bfloat16 [6144, 8192], P('cache', 'head')
- final_state: bfloat16 [48, 256, 8192], P('cache', None, 'head')
The draws below stay inside these ranges and needn't reach their ends.
Inputs may be any that keep to these rules, and one draw needn't show every extreme that they name: `owners`: within the 6 rows of one index of cache no two requests name the same owner; every owner is named by some request. `slots`: every slot is named by some request.
All inputs are finite; a program needn't handle non-finite values.
Results may differ from the reference program's by a relative error of at most 0.0039.
Values may be sent and summed in bfloat16 or wider, within the bound.
A program may use at most 256 MiB of HBM per device.

```python
import math
import jax
import jax.numpy as jnp
import numpy as np
from jax import lax

D = 8192
HEADS = 128
HEAD_DIM = 64
STATE = 256
GROUPS = 8
SUFFIX = 128
R_DEV = 6
SNAP_DEV = 8
REQUESTS = 48
TOKENS = 6144
SNAPS = 64
N_CACHE = 8


def shared_parts(key):
    common_key = jax.random.fold_in(key, 101)
    along_key = jax.random.fold_in(key, 102)
    common = jnp.clip(jax.random.normal(common_key, (D,), jnp.float32), -3.0, 3.0)
    along = jnp.clip(jax.random.normal(along_key, (GROUPS, STATE), jnp.float32), -3.0, 3.0)
    return (common, along)


def draw_tokens(key, part):
    common = shared_parts(key)[0]
    key = jax.random.fold_in(key, 21)
    amount_key, noise_key = jax.random.split(key)
    amount = jnp.clip(jax.random.normal(amount_key, (TOKENS, 1), jnp.float32), -3.0, 3.0)
    noise = jnp.clip(jax.random.normal(noise_key, (TOKENS, D), jnp.float32), -4.0, 4.0)
    values = 0.6 * amount * common[None, :] + 0.8 * noise
    return jnp.clip(values, -6.0, 6.0).astype(jnp.bfloat16)


def draw_w_bc(key, part):
    common, along = shared_parts(key)
    key = jax.random.fold_in(key, 31)
    raw = jnp.clip(jax.random.normal(key, (D, GROUPS, 2 * STATE), jnp.float32), -4.0, 4.0)
    raw = raw / math.sqrt(D)
    extra = 4.0 * common[:, None, None] * along[None, :, :] / D
    b_rows = raw[:, :, :STATE]
    c_rows = 0.01 * (raw[:, :, STATE:] + extra)
    values = jnp.concatenate([b_rows, c_rows], axis=2)
    return jnp.clip(values, -1.0, 1.0).astype(jnp.bfloat16)


def draw_pool(key, part):
    along = shared_parts(key)[1]
    key = jax.random.fold_in(key, 41)
    scale_key, noise_key = jax.random.split(key)
    width = HEADS * HEAD_DIM
    column_scale = jnp.clip(jax.random.normal(scale_key, (SNAPS, width), jnp.float32), -3.0, 3.0)
    noise = jnp.clip(jax.random.normal(noise_key, (SNAPS, STATE, width), jnp.float32), -4.0, 4.0)
    state_rows = jnp.repeat(jnp.transpose(along), width // GROUPS, axis=1)
    values = state_rows[None, :, :] * column_scale[:, None, :] + 0.5 * noise
    return jnp.clip(values, -6.0, 6.0).astype(jnp.bfloat16)


def draw_owners(key, part):
    key = jax.random.fold_in(key, 11)
    first_key, second_key = jax.random.split(key)
    half_way = N_CACHE // 2
    fixed_places = (0, 1, half_way)
    fixed_values = (N_CACHE - 1, 2, 0)
    rest_places = np.array([p for p in range(N_CACHE) if p not in fixed_places], dtype=np.int32)
    rest_values = np.array([v for v in range(N_CACHE) if v not in fixed_values], dtype=np.int32)
    shuffled = jax.random.permutation(first_key, jnp.asarray(rest_values, dtype=jnp.int32))
    base = jnp.zeros((N_CACHE,), jnp.int32).at[jnp.asarray(rest_places)].set(shuffled)
    base = base.at[0].set(N_CACHE - 1).at[1].set(2).at[half_way].set(0)
    others = jax.random.permutation(second_key, jnp.arange(N_CACHE - 1, dtype=jnp.int32)) + 1
    shifts = jnp.concatenate([jnp.zeros((1,), jnp.int32), others])[:R_DEV]
    where_to = (jnp.arange(N_CACHE, dtype=jnp.int32)[:, None] + shifts[None, :]) % N_CACHE
    return base[where_to].reshape(REQUESTS, 1).astype(jnp.int32)


def touch_ends(drawn, key, smallest, largest):
    dims = drawn.shape
    spot = [jax.random.randint(jax.random.fold_in(key, axis), (), 0, dims[axis]) for axis in range(len(dims))]
    drawn = drawn.at[tuple(spot)].set(smallest)
    longest = dims.index(max(dims))
    spot[longest] = (spot[longest] + 1) % dims[longest]
    return drawn.at[tuple(spot)].set(largest)


def block_scale(key, dims, cuts, low, high):
    def one(position, blocks):
        draws = jax.random.uniform(jax.random.fold_in(jax.random.fold_in(key, 6), position), (blocks,), jnp.float32, low / len(cuts), high / len(cuts))
        return jnp.repeat(jnp.exp(draws), dims[position] // blocks).reshape((-1,) + (1,) * (len(dims) - position - 1))

    loudness = one(*cuts[0])
    for cut in cuts[1:]:
        loudness = loudness * one(*cut)
    return loudness


def choose_distinct(rng, rows, number_of, top, lift):
    ranking = jax.random.permutation(jax.random.fold_in(rng, 1), number_of)
    pull = ranking
    for power in range(3):
        pull = pull * pull // number_of
    pull = pull * lift // number_of
    tickets = jax.random.randint(jax.random.fold_in(rng, 2), (rows, number_of), 0, 4096) + pull
    sure = jax.random.permutation(jax.random.fold_in(rng, 3), rows)[jnp.arange(number_of) % rows]
    tickets = jnp.where(jnp.arange(rows)[:, None] == sure[None, :], 1 << 14, tickets)
    merit = tickets * number_of + jnp.arange(number_of)
    return lax.top_k(merit.astype(jnp.int32), top)[1].astype(jnp.int32)


def centred(own_key, shape, deviation, bound, pieces=(), kind=jnp.bfloat16):
    values = jax.random.normal(own_key, shape, jnp.float32) * deviation
    if len(pieces) > 0:
        values = block_scale(own_key, shape, pieces, -0.22, 0.18) * values
    return jnp.clip(values, min=-bound, max=bound).astype(kind)


def setup_inputs(seed: int = 0) -> dict:
    key_of = jax.random.split(jax.random.key(seed), 12)
    return {
        "tokens": draw_tokens(jax.random.fold_in(key_of[11], 71), 0),
        "w_x": centred(key_of[1], (D, HEADS * HEAD_DIM), D ** -0.5, 0.0625, ((0, 8), (1, 4))),
        "w_bc": draw_w_bc(jax.random.fold_in(key_of[11], 71), 0),
        "w_dt": centred(key_of[3], (D, HEADS), D ** -0.5, 0.0625, ((0, 8), (1, 4))),
        "dt_bias": jnp.clip(-3.0 + 2.0 * jax.random.uniform(key_of[4], (HEADS,), jnp.float32) ** block_scale(key_of[4], (HEADS,), ((0, 4),), -0.2, 0.2), -3.0, -1.0),
        "decay_log": jnp.clip(-6.2 + 5.3999998 * jax.random.uniform(key_of[5], (HEADS,), jnp.float32) ** block_scale(key_of[5], (HEADS,), ((0, 4),), -0.2, 0.2), -6.2, -0.8),
        "skip_gain": jnp.clip(0.5 + 1.0 * jax.random.uniform(key_of[6], (HEADS,), jnp.float32) ** block_scale(key_of[6], (HEADS,), ((0, 4),), -0.2, 0.2), 0.5, 1.5),
        "pool": draw_pool(jax.random.fold_in(key_of[11], 71), 0),
        "owners": draw_owners(jax.random.fold_in(key_of[11], 71), 0),
        "slots": choose_distinct(key_of[9], REQUESTS, SNAP_DEV, 1, 0),
        "offsets": touch_ends(jax.random.randint(key_of[10], (REQUESTS,), 0, SUFFIX // 4), jax.random.fold_in(key_of[10], 1), 0, (SUFFIX // 4) - 1).astype(jnp.int32),
    }


def ssd_request(item, dt_bias, decay_log, skip_gain):
    chan, proj_bc, dt_raw, offset, start_state = item
    per_group = HEADS // GROUPS
    positions = jnp.arange(SUFFIX, dtype=jnp.int32)
    live = (positions >= offset).astype(jnp.float32)
    step = jax.nn.softplus(dt_raw + dt_bias[None, :]) * live[:, None]
    rate = -jnp.exp(decay_log)[None, :] * step
    cum = jnp.cumsum(rate, axis=0)
    b_part = proj_bc[:, :, :STATE].astype(jnp.float32)
    c_part = proj_bc[:, :, STATE:].astype(jnp.float32)
    scores = jnp.einsum("tgn,sgn->gts", c_part, b_part)
    scores = jnp.repeat(scores, per_group, axis=0)
    cum_heads = jnp.transpose(cum)
    causal = positions[:, None] >= positions[None, :]
    spread = cum_heads[:, :, None] - cum_heads[:, None, :]
    decay = jnp.where(causal[None], jnp.exp(jnp.where(causal[None], spread, 0.0)), 0.0)
    weight = (scores * decay * jnp.transpose(step)[:, None, :]).astype(jnp.bfloat16)
    chan_f = chan.astype(jnp.float32)
    inner = jnp.einsum("hts,shp->thp", weight.astype(jnp.float32), chan_f)
    state_f = start_state.astype(jnp.float32)
    carried = jnp.einsum("tgn,ngq->tgq", c_part, state_f.reshape(STATE, GROUPS, per_group * HEAD_DIM))
    carried = carried.reshape(SUFFIX, HEADS, HEAD_DIM) * jnp.exp(cum)[:, :, None]
    mixed = (inner + carried + skip_gain[None, :, None] * chan_f) * live[:, None, None]
    mixed = mixed.astype(jnp.bfloat16).reshape(SUFFIX, HEADS * HEAD_DIM)
    factor = jnp.exp(cum[-1][None, :] - cum) * step
    scaled = (chan_f * factor[:, :, None]).astype(jnp.bfloat16)
    gained = jnp.einsum("sgn,sgq->ngq", b_part, scaled.astype(jnp.float32).reshape(SUFFIX, GROUPS, per_group * HEAD_DIM))
    keep = jnp.repeat(jnp.exp(cum[-1]), HEAD_DIM)
    final_state = gained.reshape(STATE, HEADS * HEAD_DIM) + keep[None, :] * state_f
    return mixed, final_state.astype(jnp.bfloat16)


def reference(tokens, w_x, w_bc, w_dt, dt_bias, decay_log, skip_gain, pool, owners, slots, offsets):
    chan = jnp.dot(tokens, w_x, preferred_element_type=jnp.float32).astype(jnp.bfloat16)
    proj_bc = jnp.dot(tokens, w_bc.reshape(D, GROUPS * 2 * STATE), preferred_element_type=jnp.float32).astype(jnp.bfloat16)
    dt_raw = jnp.dot(tokens, w_dt, preferred_element_type=jnp.float32)
    index = (owners[:, 0] * SNAP_DEV + slots[:, 0]).astype(jnp.int32)
    start_state = jnp.take(pool, index, axis=0)
    items = (chan.reshape(REQUESTS, SUFFIX, HEADS, HEAD_DIM),
             proj_bc.reshape(REQUESTS, SUFFIX, GROUPS, 2 * STATE),
             dt_raw.reshape(REQUESTS, SUFFIX, HEADS),
             offsets, start_state)
    mixed, final_state = lax.map(lambda item: ssd_request(item, dt_bias, decay_log, skip_gain), items)
    return mixed.reshape(TOKENS, HEADS * HEAD_DIM), final_state
```

```python
import functools

import jax
import jax.numpy as jnp
from jax import lax
from jax.experimental import pallas as pl
from jax.experimental.pallas import tpu as pltpu
from jax.sharding import PartitionSpec as P

SUFFIX = 128
LANES = 128


def pick_kernel(index_ref, src_ref, out_ref):
    del index_ref
    width = out_ref.shape[-1]
    for part in range(out_ref.shape[1]):
        out_ref[0, part] = src_ref[0, :, part * width : (part + 1) * width]


def pick_for_owners(pool, chosen, parts):
    count = chosen.shape[0]
    _, rows, cols = pool.shape
    width = cols // parts
    return pl.pallas_call(
        pick_kernel,
        out_shape=jax.ShapeDtypeStruct((count, parts, rows, width), pool.dtype),
        grid_spec=pltpu.PrefetchScalarGridSpec(
            num_scalar_prefetch=1,
            grid=(count,),
            in_specs=[pl.BlockSpec((1, rows, cols), lambda i, s: (s[i], 0, 0))],
            out_specs=pl.BlockSpec((1, parts, rows, width), lambda i, s: (i, 0, 0, 0)),
        ),
        cost_estimate=pl.CostEstimate(
            flops=0, bytes_accessed=4 * count * rows * cols, transcendentals=0
        ),
    )(chosen, pool)


def turn_kernel(index_ref, src_ref, out_ref):
    del index_ref
    out_ref[:, 0] = src_ref[0]


def pick_for_requests(received, my_owners):
    count = my_owners.shape[0]
    _, parts, rows, width = received.shape
    return pl.pallas_call(
        turn_kernel,
        out_shape=jax.ShapeDtypeStruct((parts, count, rows, width), received.dtype),
        grid_spec=pltpu.PrefetchScalarGridSpec(
            num_scalar_prefetch=1,
            grid=(count,),
            in_specs=[pl.BlockSpec((1, parts, rows, width), lambda i, s: (s[i], 0, 0, 0))],
            out_specs=pl.BlockSpec((parts, 1, rows, width), lambda i, s: (0, i, 0, 0)),
        ),
        cost_estimate=pl.CostEstimate(
            flops=0, bytes_accessed=4 * count * parts * rows * width, transcendentals=0
        ),
    )(my_owners, received)


def ssd_kernel(first, heads, width, n_carry, *refs):
    (chan_ref, bc_ref, cum_ref, cum_t_ref, step_t_ref, factor_ref, grown_ref, live_ref,
     keep_ref, gain_ref, state_ref) = refs[:11]
    mixed_ref, final_ref, scaled_ref = refs[11 + n_carry :]
    state_size = bc_ref.shape[1] // 2
    b_part = bc_ref[:, :state_size]
    c_part = bc_ref[:, state_size:]
    scores = lax.dot_general(
        c_part, b_part, (((1,), (1,)), ((), ())), preferred_element_type=jnp.float32
    )
    state = state_ref[...].reshape(state_size, heads * width)
    carried = jnp.dot(c_part, state, preferred_element_type=jnp.float32)
    here = lax.broadcasted_iota(jnp.int32, (SUFFIX, SUFFIX), 0)
    there = lax.broadcasted_iota(jnp.int32, (SUFFIX, SUFFIX), 1)
    causal = here >= there
    per_tile = LANES // width
    lane_head = lax.broadcasted_iota(jnp.int32, (SUFFIX, LANES), 1) // width
    live = live_ref[...]

    def spread_heads(ref, head):
        value = jnp.broadcast_to(ref[:, head : head + 1], (SUFFIX, LANES))
        for k in range(1, per_tile):
            value = jnp.where(lane_head == k, ref[:, head + k : head + k + 1], value)
        return value

    for tile in range(heads // per_tile):
        head = first + tile * per_tile
        lanes = slice(tile * LANES, (tile + 1) * LANES)
        chan = chan_ref[:, lanes].astype(jnp.float32)
        weights, values = [], []
        for k in range(per_tile):
            h = head + k
            spread = cum_ref[:, h : h + 1] - cum_t_ref[0, h : h + 1, :]
            decay = jnp.exp(jnp.where(causal, spread, -1e30))
            weights.append((scores * decay * step_t_ref[0, h : h + 1, :]).astype(jnp.bfloat16))
            values.append(jnp.where(lane_head == k, chan, 0.0).astype(jnp.bfloat16))
        inner = jnp.dot(
            jnp.concatenate(weights, axis=1),
            jnp.concatenate(values, axis=0),
            preferred_element_type=jnp.float32,
        )
        mixed = inner + carried[:, lanes] * spread_heads(grown_ref, head)
        mixed = (mixed + gain_ref[:, lanes] * chan) * live
        mixed_ref[:, lanes] = mixed.astype(jnp.bfloat16)
        scaled_ref[:, lanes] = (chan * spread_heads(factor_ref, head)).astype(jnp.bfloat16)
    gained = lax.dot_general(
        b_part, scaled_ref[...], (((0,), (0,)), ((), ())), preferred_element_type=jnp.float32
    )
    final_ref[0] = (gained + keep_ref[0] * state.astype(jnp.float32)).astype(jnp.bfloat16)


def ssd(first, heads, group, chan, proj_bc, small, state, carry, total_cols):
    cum, cum_t, step_t, factor, grown, live, keep, gain = small
    tokens, cols = chan.shape
    requests = tokens // SUFFIX
    all_heads = cum.shape[1]
    parts, _, rows, _ = state.shape
    state_size = parts * rows
    width = cols // heads
    block = first * width // cols
    in_specs = [
        pl.BlockSpec((SUFFIX, cols), lambda r: (r, 0)),
        pl.BlockSpec((SUFFIX, 2 * state_size), lambda r: (r, group)),
        pl.BlockSpec((SUFFIX, all_heads), lambda r: (r, 0)),
        pl.BlockSpec((1, all_heads, SUFFIX), lambda r: (r, 0, 0)),
        pl.BlockSpec((1, all_heads, SUFFIX), lambda r: (r, 0, 0)),
        pl.BlockSpec((SUFFIX, all_heads), lambda r: (r, 0)),
        pl.BlockSpec((SUFFIX, all_heads), lambda r: (r, 0)),
        pl.BlockSpec((SUFFIX, 1), lambda r: (r, 0)),
        pl.BlockSpec((1, 1, cols), lambda r: (r, 0, block)),
        pl.BlockSpec((1, cols), lambda r: (0, block)),
        pl.BlockSpec((parts, 1, rows, cols), lambda r: (0, r, 0, block)),
    ]
    aliases = {}
    if carry:
        in_specs += [pl.BlockSpec(memory_space=pl.ANY)] * len(carry)
        aliases = {11 + i: i for i in range(len(carry))}
    flops = 2 * tokens * cols * (2 * state_size + 2 * SUFFIX)
    return pl.pallas_call(
        functools.partial(ssd_kernel, first, heads, width, len(carry)),
        out_shape=(
            jax.ShapeDtypeStruct((tokens, total_cols), jnp.bfloat16),
            jax.ShapeDtypeStruct((requests, state_size, total_cols), jnp.bfloat16),
        ),
        grid=(requests,),
        in_specs=in_specs,
        out_specs=(
            pl.BlockSpec((SUFFIX, cols), lambda r: (r, block)),
            pl.BlockSpec((1, state_size, cols), lambda r: (r, 0, block)),
        ),
        scratch_shapes=[pltpu.VMEM((SUFFIX, cols), jnp.bfloat16)],
        input_output_aliases=aliases,
        compiler_params=pltpu.CompilerParams(vmem_limit_bytes=48 * 1024 * 1024),
        cost_estimate=pl.CostEstimate(
            flops=flops,
            bytes_accessed=4 * cols * (tokens + requests * state_size),
            transcendentals=tokens * SUFFIX * heads,
        ),
    )(chan, proj_bc, cum, cum_t, step_t, factor, grown, live, keep, gain, state, *carry)


def body(tokens, w_x, w_bc, w_dt, dt_bias, decay_log, skip_gain, pool, owners, slots, offsets):
    token_count = tokens.shape[0]
    requests_here = token_count // SUFFIX
    heads_here = dt_bias.shape[0]
    groups_here = w_bc.shape[1]
    per_group = heads_here // groups_here
    total_cols = w_x.shape[1]
    head_width = total_cols // heads_here
    bc_cols = w_bc.shape[1] * w_bc.shape[2]
    cache_count = lax.axis_size("cache")
    head_count = lax.axis_size("head")
    my_cache = lax.axis_index("cache")

    chunks = []
    for group in range(groups_here):
        pieces = 2 if group == groups_here - 1 else 1
        size = per_group // pieces
        chunks += [(group * per_group + i * size, size, group) for i in range(pieces)]

    local_small = jnp.concatenate([w_bc.reshape(w_bc.shape[0], bc_cols), w_dt], axis=1)
    w_small = lax.all_gather(local_small, "cache", axis=0, tiled=True)
    w_parts = [
        lax.all_gather(
            w_x[:, first * head_width : (first + size) * head_width], "cache", axis=0, tiled=True
        )
        for first, size, _ in chunks
    ]

    owner_table = owners[:, 0].reshape(cache_count, requests_here)
    slot_table = slots[:, 0].reshape(cache_count, requests_here)
    chosen_slot = jnp.sum(jnp.where(owner_table == my_cache, slot_table, 0), axis=1)
    my_owners = lax.dynamic_slice_in_dim(owners[:, 0], my_cache * requests_here, requests_here)
    blocks = pick_for_owners(pool, chosen_slot, head_count)
    received = lax.all_to_all(blocks, "cache", split_axis=0, concat_axis=0, tiled=True)
    wanted = pick_for_requests(received, my_owners)
    state = lax.all_to_all(wanted, "head", split_axis=0, concat_axis=0, tiled=True)

    part_small = jnp.dot(tokens, w_small, preferred_element_type=jnp.float32)
    proj_bc = part_small[:, :bc_cols].astype(jnp.bfloat16)
    dt_raw = part_small[:, bc_cols:].reshape(requests_here, SUFFIX, heads_here)
    positions = jnp.arange(SUFFIX, dtype=jnp.int32)
    live = (positions[None, :] >= offsets[:, None]).astype(jnp.float32)
    step = jax.nn.softplus(dt_raw + dt_bias[None, None, :]) * live[:, :, None]
    rate = -jnp.exp(decay_log)[None, None, :] * step
    cum = jnp.cumsum(rate, axis=1)
    last = cum[:, -1:, :]
    factor = jnp.exp(last - cum) * step
    small = (
        cum.reshape(token_count, heads_here),
        jnp.transpose(cum, (0, 2, 1)),
        jnp.transpose(step, (0, 2, 1)),
        factor.reshape(token_count, heads_here),
        jnp.exp(cum).reshape(token_count, heads_here),
        live.reshape(token_count, 1),
        jnp.repeat(jnp.exp(last), head_width, axis=2),
        jnp.repeat(skip_gain, head_width)[None, :],
    )

    carry = ()
    for (first, size, group), w_part in zip(chunks, w_parts):
        chan = jnp.dot(tokens, w_part, preferred_element_type=jnp.float32).astype(jnp.bfloat16)
        carry = ssd(first, size, group, chan, proj_bc, small, state, carry, total_cols)
    return tuple(carry)


def solution(mesh):
    return jax.shard_map(
        body,
        mesh=mesh,
        in_specs=(
            P("cache", None),
            P("cache", "head"),
            P("cache", "head", None),
            P("cache", "head"),
            P("head"),
            P("head"),
            P("head"),
            P("cache", "head", None),
            P(),
            P(),
            P("cache"),
        ),
        out_specs=(P("cache", "head"), P("cache", None, "head")),
        check_vma=False,
    )
```

```python
import functools

import jax
import jax.numpy as jnp
from jax import lax
from jax.experimental import pallas as pl
from jax.experimental.pallas import tpu as pltpu
from jax.sharding import PartitionSpec as P

SUFFIX = 128
LANES = 128


def pick_kernel(index_ref, src_ref, out_ref):
    del index_ref
    width = out_ref.shape[-1]
    for part in range(out_ref.shape[1]):
        out_ref[0, part] = src_ref[0, :, part * width : (part + 1) * width]


def pick_for_owners(pool, chosen, parts):
    count = chosen.shape[0]
    _, rows, cols = pool.shape
    width = cols // parts
    return pl.pallas_call(
        pick_kernel,
        out_shape=jax.ShapeDtypeStruct((count, parts, rows, width), pool.dtype),
        grid_spec=pltpu.PrefetchScalarGridSpec(
            num_scalar_prefetch=1,
            grid=(count,),
            in_specs=[pl.BlockSpec((1, rows, cols), lambda i, s: (s[i], 0, 0))],
            out_specs=pl.BlockSpec((1, parts, rows, width), lambda i, s: (i, 0, 0, 0)),
        ),
        cost_estimate=pl.CostEstimate(
            flops=0, bytes_accessed=4 * count * rows * cols, transcendentals=0
        ),
    )(chosen, pool)


def turn_kernel(index_ref, src_ref, out_ref):
    del index_ref
    out_ref[:, 0] = src_ref[0]


def pick_for_requests(received, my_owners):
    count = my_owners.shape[0]
    _, parts, rows, width = received.shape
    return pl.pallas_call(
        turn_kernel,
        out_shape=jax.ShapeDtypeStruct((parts, count, rows, width), received.dtype),
        grid_spec=pltpu.PrefetchScalarGridSpec(
            num_scalar_prefetch=1,
            grid=(count,),
            in_specs=[pl.BlockSpec((1, parts, rows, width), lambda i, s: (s[i], 0, 0, 0))],
            out_specs=pl.BlockSpec((parts, 1, rows, width), lambda i, s: (0, i, 0, 0)),
        ),
        cost_estimate=pl.CostEstimate(
            flops=0, bytes_accessed=4 * count * parts * rows * width, transcendentals=0
        ),
    )(my_owners, received)


def ssd_kernel(first, heads, width, n_carry, index_ref, *refs):
    del index_ref
    (chan_ref, bc_ref, cum_ref, cum_t_ref, step_t_ref, factor_ref, grown_ref, live_ref,
     keep_ref, gain_ref, state_ref) = refs[:11]
    mixed_ref, final_ref, scaled_ref = refs[11 + n_carry :]
    state_size = bc_ref.shape[1] // 2
    b_part = bc_ref[:, :state_size]
    c_part = bc_ref[:, state_size:]
    scores = lax.dot_general(
        c_part, b_part, (((1,), (1,)), ((), ())), preferred_element_type=jnp.float32
    )
    state = state_ref[...].reshape(state_size, heads * width)
    carried = jnp.dot(c_part, state, preferred_element_type=jnp.float32)
    here = lax.broadcasted_iota(jnp.int32, (SUFFIX, SUFFIX), 0)
    there = lax.broadcasted_iota(jnp.int32, (SUFFIX, SUFFIX), 1)
    causal = here >= there
    per_tile = LANES // width
    lane_head = lax.broadcasted_iota(jnp.int32, (SUFFIX, LANES), 1) // width
    live = live_ref[...]

    def spread_heads(ref, head):
        value = jnp.broadcast_to(ref[:, head : head + 1], (SUFFIX, LANES))
        for k in range(1, per_tile):
            value = jnp.where(lane_head == k, ref[:, head + k : head + k + 1], value)
        return value

    for tile in range(heads // per_tile):
        head = first + tile * per_tile
        lanes = slice(tile * LANES, (tile + 1) * LANES)
        chan = chan_ref[:, lanes].astype(jnp.float32)
        weights, values = [], []
        for k in range(per_tile):
            h = head + k
            spread = cum_ref[:, h : h + 1] - cum_t_ref[0, h : h + 1, :]
            decay = jnp.exp(jnp.where(causal, spread, -1e30))
            weights.append((scores * decay * step_t_ref[0, h : h + 1, :]).astype(jnp.bfloat16))
            values.append(jnp.where(lane_head == k, chan, 0.0).astype(jnp.bfloat16))
        inner = jnp.dot(
            jnp.concatenate(weights, axis=1),
            jnp.concatenate(values, axis=0),
            preferred_element_type=jnp.float32,
        )
        mixed = inner + carried[:, lanes] * spread_heads(grown_ref, head)
        mixed = (mixed + gain_ref[:, lanes] * chan) * live
        mixed_ref[:, lanes] = mixed.astype(jnp.bfloat16)
        scaled_ref[:, lanes] = (chan * spread_heads(factor_ref, head)).astype(jnp.bfloat16)
    gained = lax.dot_general(
        b_part, scaled_ref[...], (((0,), (0,)), ((), ())), preferred_element_type=jnp.float32
    )
    final_ref[0] = (gained + keep_ref[0] * state.astype(jnp.float32)).astype(jnp.bfloat16)


def ssd(first, heads, group, chan, proj_bc, small, state, places, carry, total_cols):
    cum, cum_t, step_t, factor, grown, live, keep, gain = small
    tokens = chan.shape[0]
    requests = tokens // SUFFIX
    all_heads = cum.shape[1]
    parts, _, rows, _ = state.shape
    state_size = parts * rows
    width = total_cols // all_heads
    cols = heads * width
    block = first * width // cols
    chan_block = block if chan.shape[1] == total_cols else 0
    in_specs = [
        pl.BlockSpec((SUFFIX, cols), lambda r, s: (r, chan_block)),
        pl.BlockSpec((SUFFIX, 2 * state_size), lambda r, s: (r, group)),
        pl.BlockSpec((SUFFIX, all_heads), lambda r, s: (r, 0)),
        pl.BlockSpec((1, all_heads, SUFFIX), lambda r, s: (r, 0, 0)),
        pl.BlockSpec((1, all_heads, SUFFIX), lambda r, s: (r, 0, 0)),
        pl.BlockSpec((SUFFIX, all_heads), lambda r, s: (r, 0)),
        pl.BlockSpec((SUFFIX, all_heads), lambda r, s: (r, 0)),
        pl.BlockSpec((SUFFIX, 1), lambda r, s: (r, 0)),
        pl.BlockSpec((1, 1, cols), lambda r, s: (r, 0, block)),
        pl.BlockSpec((1, cols), lambda r, s: (0, block)),
        pl.BlockSpec((parts, 1, rows, cols), lambda r, s: (0, s[r], 0, block)),
    ]
    aliases = {}
    if carry:
        in_specs += [pl.BlockSpec(memory_space=pl.ANY)] * len(carry)
        aliases = {12 + i: i for i in range(len(carry))}
    flops = 2 * tokens * cols * (2 * state_size + 2 * SUFFIX)
    return pl.pallas_call(
        functools.partial(ssd_kernel, first, heads, width, len(carry)),
        out_shape=(
            jax.ShapeDtypeStruct((tokens, total_cols), jnp.bfloat16),
            jax.ShapeDtypeStruct((requests, state_size, total_cols), jnp.bfloat16),
        ),
        grid_spec=pltpu.PrefetchScalarGridSpec(
            num_scalar_prefetch=1,
            grid=(requests,),
            in_specs=in_specs,
            out_specs=(
                pl.BlockSpec((SUFFIX, cols), lambda r, s: (r, block)),
                pl.BlockSpec((1, state_size, cols), lambda r, s: (r, 0, block)),
            ),
            scratch_shapes=[pltpu.VMEM((SUFFIX, cols), jnp.bfloat16)],
        ),
        input_output_aliases=aliases,
        compiler_params=pltpu.CompilerParams(vmem_limit_bytes=48 * 1024 * 1024),
        cost_estimate=pl.CostEstimate(
            flops=flops,
            bytes_accessed=4 * cols * (tokens + requests * state_size),
            transcendentals=tokens * SUFFIX * heads,
        ),
    )(places, chan, proj_bc, cum, cum_t, step_t, factor, grown, live, keep, gain, state, *carry)


MESH = pl.DeviceIdType.MESH


def flip(index, bits):
    result = index
    for bit in (1, 2, 4):
        if bits & bit:
            result = result + bit - 2 * bit * ((index // bit) % 2)
    return result


def project(tokens_vmem, w_ref, out_ref, total, tile):
    depth, cols = w_ref.shape
    rows = tokens_vmem.shape[0]
    k_tile = min(depth, 2048)
    steps = depth // k_tile

    def step(w_block, out_block):
        k = pl.program_id(1)
        columns = pl.ds(pl.multiple_of(k * k_tile, k_tile), k_tile)
        part = jnp.dot(
            tokens_vmem[:, columns], w_block[...], preferred_element_type=jnp.float32
        )

        @pl.when(k == 0)
        def _():
            total[:, :tile] = part

        @pl.when(k > 0)
        def _():
            total[:, :tile] += part

        @pl.when(k == steps - 1)
        def _():
            out_block[...] = total[:, :tile].astype(out_block.dtype)

    pltpu.emit_pipeline(
        step,
        grid=(cols // tile, steps),
        in_specs=[pl.BlockSpec((k_tile, tile), lambda n, k: (k, n))],
        out_specs=[pl.BlockSpec((rows, tile), lambda n, k: (0, n))],
    )(w_ref, out_ref)


def exchange_kernel(bc_cols, tile, tokens_ref, small_ref, x_ref, blocks_ref, chan_ref, proj_ref, dt_ref,
                    w_small, w_all, landed, state_ref, tokens_vmem, total, w_send, w_recv, w_here,
                    snap_send, snap_recv, z_send, z_recv, z_here, tokens_sem):
    me, my_z = lax.axis_index("cache"), lax.axis_index("head")
    n_cache, n_head = blocks_ref.shape[0], blocks_ref.shape[1]
    depth = small_ref.shape[0]
    half = depth // 2

    barrier = pltpu.get_barrier_semaphore()
    for a in range(1, n_cache):
        pl.semaphore_signal(barrier, inc=1, device_id=(flip(me, a), my_z), device_id_type=MESH)
    for b in range(1, n_head):
        pl.semaphore_signal(barrier, inc=1, device_id=(me, flip(my_z, b)), device_id_type=MESH)
    pl.semaphore_wait(barrier, n_cache + n_head - 2)

    chunks = [(small_ref, w_small, 0, small_ref.shape[1])]
    chunks += [(x_ref, w_all, c, tile) for c in range(0, x_ref.shape[1], tile)]

    def remote(src, dst, sends, recvs, index, device):
        return pltpu.make_async_remote_copy(
            src_ref=src, dst_ref=dst, send_sem=sends.at[index], recv_sem=recvs.at[index],
            device_id=device, device_id_type=MESH,
        )

    def weights(i, kind):
        src, dst, first, width = chunks[i]
        to, owner, low, rows = (
            (2, 0, 0, depth), (4, 0, 0, depth), (1, 0, 0, depth),
            (4, 2, 0, half), (1, 2, 0, depth), (2, 4, half, half), (1, 4, 0, depth),
            (1, 6, 0, half), (1, 6, half, half),
        )[kind]
        columns = pl.ds(first, width)
        place = dst.at[pl.ds(pl.multiple_of(flip(me, owner) * depth, depth) + low, rows), columns]
        source = src.at[:, columns] if kind < 3 else place
        return remote(source, place, w_send, w_recv, (i, kind), (flip(me, to), my_z))

    def own(i):
        src, dst, first, width = chunks[i]
        columns = pl.ds(first, width)
        rows = pl.ds(pl.multiple_of(me * depth, depth), depth)
        return pltpu.make_async_copy(src.at[:, columns], dst.at[rows, columns], w_here.at[i])

    def snapshot(a):
        peer = flip(me, a)
        return remote(blocks_ref.at[peer], landed.at[me], snap_send, snap_recv, (a - 1,), (peer, my_z))

    def along_z(a, b):
        peer = flip(me, a)
        to = flip(my_z, b)
        src = (landed if a else blocks_ref).at[peer, to]
        if b == 0:
            return pltpu.make_async_copy(src, state_ref.at[my_z, peer], z_here.at[a])
        return remote(src, state_ref.at[my_z, peer], z_send, z_recv, (a, b - 1), (me, to))

    count = len(chunks)
    tokens_copy = pltpu.make_async_copy(tokens_ref, tokens_vmem, tokens_sem)

    def start_direct(i):
        for kind in range(3):
            weights(i, kind).start()
        own(i).start()

    def arrive_direct(i):
        weights(i, 0).wait_recv()
        weights(i, 3).start()
        weights(i, 4).start()
        weights(i, 1).wait_recv()
        weights(i, 5).start()
        weights(i, 6).start()

    def arrive_diagonal(i):
        weights(i, 3).wait_recv()
        weights(i, 7).start()
        weights(i, 5).wait_recv()
        weights(i, 8).start()

    def arrive_rest(i):
        own(i).wait()
        for kind in (2, 4, 6, 7, 8):
            weights(i, kind).wait_recv()

    def multiply(i):
        if i == 0:
            project(tokens_vmem, w_small.at[:, :bc_cols], proj_ref, total, min(tile, bc_cols))
            project(tokens_vmem, w_small.at[:, bc_cols:], dt_ref, total, LANES)
        else:
            columns = pl.ds(chunks[i][2], tile)
            project(tokens_vmem, w_all.at[:, columns], chan_ref.at[:, columns], total, tile)

    for b in (1, 2, 3, 0):
        along_z(0, b).start()
    for a in (1, 2, 4, 3, 5, 6, 7):
        snapshot(a).start()
    start_direct(0)
    tokens_copy.start()
    start_direct(1)
    for a in (1, 2, 4, 3, 5, 6, 7):
        snapshot(a).wait_recv()
        for b in (1, 2, 3, 0):
            along_z(a, b).start()
    tokens_copy.wait()
    for i in range(count + 1):
        if i < count:
            arrive_direct(i)
            if i + 2 < count:
                start_direct(i + 2)
        if i >= 1:
            arrive_diagonal(i - 1)
            arrive_rest(i - 1)
            multiply(i - 1)
    for a in range(n_cache):
        along_z(a, 0).wait()
        for b in range(1, n_head):
            along_z(a, b).wait()
    for a in range(1, n_cache):
        snapshot(a).wait_send()
    for i in range(count):
        for kind in range(9):
            weights(i, kind).wait_send()


def exchange(tokens, local_small, w_x, blocks, bc_cols):
    rows, model = tokens.shape
    n_cache, n_head, state_rows, width = blocks.shape
    small_cols, cols = local_small.shape[1], w_x.shape[1]
    tile = 512
    count = 1 + cols // tile
    bf16 = jnp.bfloat16
    anywhere = pl.BlockSpec(memory_space=pl.ANY)
    dma = pltpu.SemaphoreType.DMA
    outs = pl.pallas_call(
        functools.partial(exchange_kernel, bc_cols, tile),
        out_shape=(
            jax.ShapeDtypeStruct((rows, cols), bf16),
            jax.ShapeDtypeStruct((rows, bc_cols), bf16),
            jax.ShapeDtypeStruct((rows, small_cols - bc_cols), jnp.float32),
            jax.ShapeDtypeStruct((model, small_cols), bf16),
            jax.ShapeDtypeStruct((model, cols), bf16),
            jax.ShapeDtypeStruct(blocks.shape, bf16),
            jax.ShapeDtypeStruct((n_head, n_cache, state_rows, width), bf16),
        ),
        in_specs=[anywhere] * 4,
        out_specs=[anywhere] * 7,
        scratch_shapes=[
            pltpu.VMEM(tokens.shape, bf16),
            pltpu.VMEM((rows, tile), jnp.float32),
            dma((count, 9)),
            dma((count, 9)),
            dma((count,)),
            dma((n_cache - 1,)),
            dma((n_cache - 1,)),
            dma((n_cache, n_head - 1)),
            dma((n_cache, n_head - 1)),
            dma((n_cache,)),
            dma,
        ],
        compiler_params=pltpu.CompilerParams(
            collective_id=0, has_side_effects=True, vmem_limit_bytes=48 * 1024 * 1024
        ),
        cost_estimate=pl.CostEstimate(
            flops=2 * rows * model * (cols + small_cols),
            bytes_accessed=4 * model * (cols + small_cols),
            transcendentals=0,
        ),
    )(tokens, local_small, w_x, blocks)
    return outs[0], outs[1], outs[2], outs[6]


def body(tokens, w_x, w_bc, w_dt, dt_bias, decay_log, skip_gain, pool, owners, slots, offsets):
    token_count = tokens.shape[0]
    requests_here = token_count // SUFFIX
    heads_here = dt_bias.shape[0]
    groups_here = w_bc.shape[1]
    per_group = heads_here // groups_here
    total_cols = w_x.shape[1]
    head_width = total_cols // heads_here
    bc_cols = w_bc.shape[1] * w_bc.shape[2]
    cache_count = lax.axis_size("cache")
    head_count = lax.axis_size("head")
    my_cache = lax.axis_index("cache")

    one_kernel = cache_count == 8 and head_count == 4
    chunks = []
    for group in range(groups_here):
        pieces = 2 if group == groups_here - 1 and not one_kernel else 1
        size = per_group // pieces
        chunks += [(group * per_group + i * size, size, group) for i in range(pieces)]

    pad = -w_dt.shape[1] % LANES
    local_small = jnp.concatenate(
        [w_bc.reshape(w_bc.shape[0], bc_cols), jnp.pad(w_dt, ((0, 0), (0, pad)))], axis=1
    )
    owner_table = owners[:, 0].reshape(cache_count, requests_here)
    slot_table = slots[:, 0].reshape(cache_count, requests_here)
    chosen_slot = jnp.sum(jnp.where(owner_table == my_cache, slot_table, 0), axis=1)
    my_owners = lax.dynamic_slice_in_dim(owners[:, 0], my_cache * requests_here, requests_here)
    blocks = pick_for_owners(pool, chosen_slot, head_count)

    if one_kernel:
        chan_all, proj_bc, part_dt, state = exchange(tokens, local_small, w_x, blocks, bc_cols)
        places = my_owners
    else:
        w_small = lax.all_gather(local_small, "cache", axis=0, tiled=True)
        w_parts = [
            lax.all_gather(
                w_x[:, first * head_width : (first + size) * head_width],
                "cache",
                axis=0,
                tiled=True,
            )
            for first, size, _ in chunks
        ]
        received = lax.all_to_all(blocks, "cache", split_axis=0, concat_axis=0, tiled=True)
        wanted = pick_for_requests(received, my_owners)
        state = lax.all_to_all(wanted, "head", split_axis=0, concat_axis=0, tiled=True)
        places = jnp.arange(requests_here, dtype=jnp.int32)
        part_small = jnp.dot(tokens, w_small, preferred_element_type=jnp.float32)
        proj_bc = part_small[:, :bc_cols].astype(jnp.bfloat16)
        part_dt = part_small[:, bc_cols:]
    dt_raw = part_dt[:, :heads_here].reshape(requests_here, SUFFIX, heads_here)
    positions = jnp.arange(SUFFIX, dtype=jnp.int32)
    live = (positions[None, :] >= offsets[:, None]).astype(jnp.float32)
    step = jax.nn.softplus(dt_raw + dt_bias[None, None, :]) * live[:, :, None]
    rate = -jnp.exp(decay_log)[None, None, :] * step
    cum = jnp.cumsum(rate, axis=1)
    last = cum[:, -1:, :]
    factor = jnp.exp(last - cum) * step
    small = (
        cum.reshape(token_count, heads_here),
        jnp.transpose(cum, (0, 2, 1)),
        jnp.transpose(step, (0, 2, 1)),
        factor.reshape(token_count, heads_here),
        jnp.exp(cum).reshape(token_count, heads_here),
        live.reshape(token_count, 1),
        jnp.repeat(jnp.exp(last), head_width, axis=2),
        jnp.repeat(skip_gain, head_width)[None, :],
    )

    carry = ()
    for place, (first, size, group) in enumerate(chunks):
        if one_kernel:
            chan = chan_all
        else:
            chan = jnp.dot(tokens, w_parts[place], preferred_element_type=jnp.float32)
            chan = chan.astype(jnp.bfloat16)
        carry = ssd(
            first, size, group, chan, proj_bc, small, state, places, carry, total_cols
        )
    return tuple(carry)


def solution(mesh):
    return jax.shard_map(
        body,
        mesh=mesh,
        in_specs=(
            P("cache", None),
            P("cache", "head"),
            P("cache", "head", None),
            P("cache", "head"),
            P("head"),
            P("head"),
            P("head"),
            P("cache", "head", None),
            P(),
            P(),
            P("cache"),
        ),
        out_specs=(P("cache", "head"), P("cache", None, "head")),
        check_vma=False,
    )
```

```python
import functools

import jax
import jax.numpy as jnp
from jax import lax
from jax.experimental import pallas as pl
from jax.experimental.pallas import tpu as pltpu
from jax.sharding import PartitionSpec as P

SUFFIX = 128
LANES = 128


def pick_kernel(index_ref, src_ref, out_ref):
    del index_ref
    width = out_ref.shape[-1]
    for part in range(out_ref.shape[1]):
        out_ref[0, part] = src_ref[0, :, part * width : (part + 1) * width]


def pick_for_owners(pool, chosen, parts):
    count = chosen.shape[0]
    _, rows, cols = pool.shape
    width = cols // parts
    return pl.pallas_call(
        pick_kernel,
        out_shape=jax.ShapeDtypeStruct((count, parts, rows, width), pool.dtype),
        grid_spec=pltpu.PrefetchScalarGridSpec(
            num_scalar_prefetch=1,
            grid=(count,),
            in_specs=[pl.BlockSpec((1, rows, cols), lambda i, s: (s[i], 0, 0))],
            out_specs=pl.BlockSpec((1, parts, rows, width), lambda i, s: (i, 0, 0, 0)),
        ),
        cost_estimate=pl.CostEstimate(
            flops=0, bytes_accessed=4 * count * rows * cols, transcendentals=0
        ),
    )(chosen, pool)


def turn_kernel(index_ref, src_ref, out_ref):
    del index_ref
    out_ref[:, 0] = src_ref[0]


def pick_for_requests(received, my_owners):
    count = my_owners.shape[0]
    _, parts, rows, width = received.shape
    return pl.pallas_call(
        turn_kernel,
        out_shape=jax.ShapeDtypeStruct((parts, count, rows, width), received.dtype),
        grid_spec=pltpu.PrefetchScalarGridSpec(
            num_scalar_prefetch=1,
            grid=(count,),
            in_specs=[pl.BlockSpec((1, parts, rows, width), lambda i, s: (s[i], 0, 0, 0))],
            out_specs=pl.BlockSpec((parts, 1, rows, width), lambda i, s: (0, i, 0, 0)),
        ),
        cost_estimate=pl.CostEstimate(
            flops=0, bytes_accessed=4 * count * parts * rows * width, transcendentals=0
        ),
    )(my_owners, received)


def ssd_kernel(first, heads, width, n_carry, index_ref, *refs):
    del index_ref
    (chan_ref, bc_ref, cum_ref, cum_t_ref, step_t_ref, factor_ref, grown_ref, live_ref,
     keep_ref, gain_ref, state_ref) = refs[:11]
    mixed_ref, final_ref, scaled_ref = refs[11 + n_carry :]
    state_size = bc_ref.shape[1] // 2
    b_part = bc_ref[:, :state_size]
    c_part = bc_ref[:, state_size:]
    scores = lax.dot_general(
        c_part, b_part, (((1,), (1,)), ((), ())), preferred_element_type=jnp.float32
    )
    state = state_ref[...].reshape(state_size, heads * width)
    carried = jnp.dot(c_part, state, preferred_element_type=jnp.float32)
    here = lax.broadcasted_iota(jnp.int32, (SUFFIX, SUFFIX), 0)
    there = lax.broadcasted_iota(jnp.int32, (SUFFIX, SUFFIX), 1)
    causal = here >= there
    per_tile = LANES // width
    lane_head = lax.broadcasted_iota(jnp.int32, (SUFFIX, LANES), 1) // width
    live = live_ref[...]

    def spread_heads(ref, head):
        value = jnp.broadcast_to(ref[:, head : head + 1], (SUFFIX, LANES))
        for k in range(1, per_tile):
            value = jnp.where(lane_head == k, ref[:, head + k : head + k + 1], value)
        return value

    for tile in range(heads // per_tile):
        head = first + tile * per_tile
        lanes = slice(tile * LANES, (tile + 1) * LANES)
        chan = chan_ref[:, lanes].astype(jnp.float32)
        weights, values = [], []
        for k in range(per_tile):
            h = head + k
            spread = cum_ref[:, h : h + 1] - cum_t_ref[0, h : h + 1, :]
            decay = jnp.exp(jnp.where(causal, spread, -1e30))
            weights.append((scores * decay * step_t_ref[0, h : h + 1, :]).astype(jnp.bfloat16))
            values.append(jnp.where(lane_head == k, chan, 0.0).astype(jnp.bfloat16))
        inner = jnp.dot(
            jnp.concatenate(weights, axis=1),
            jnp.concatenate(values, axis=0),
            preferred_element_type=jnp.float32,
        )
        mixed = inner + carried[:, lanes] * spread_heads(grown_ref, head)
        mixed = (mixed + gain_ref[:, lanes] * chan) * live
        mixed_ref[:, lanes] = mixed.astype(jnp.bfloat16)
        scaled_ref[:, lanes] = (chan * spread_heads(factor_ref, head)).astype(jnp.bfloat16)
    gained = lax.dot_general(
        b_part, scaled_ref[...], (((0,), (0,)), ((), ())), preferred_element_type=jnp.float32
    )
    final_ref[0] = (gained + keep_ref[0] * state.astype(jnp.float32)).astype(jnp.bfloat16)


def ssd(first, heads, group, chan, proj_bc, small, state, places, carry, total_cols):
    cum, cum_t, step_t, factor, grown, live, keep, gain = small
    tokens = chan.shape[0]
    requests = tokens // SUFFIX
    all_heads = cum.shape[1]
    parts, _, rows, _ = state.shape
    state_size = parts * rows
    width = total_cols // all_heads
    cols = heads * width
    block = first * width // cols
    chan_block = block if chan.shape[1] == total_cols else 0
    in_specs = [
        pl.BlockSpec((SUFFIX, cols), lambda r, s: (r, chan_block)),
        pl.BlockSpec((SUFFIX, 2 * state_size), lambda r, s: (r, group)),
        pl.BlockSpec((SUFFIX, all_heads), lambda r, s: (r, 0)),
        pl.BlockSpec((1, all_heads, SUFFIX), lambda r, s: (r, 0, 0)),
        pl.BlockSpec((1, all_heads, SUFFIX), lambda r, s: (r, 0, 0)),
        pl.BlockSpec((SUFFIX, all_heads), lambda r, s: (r, 0)),
        pl.BlockSpec((SUFFIX, all_heads), lambda r, s: (r, 0)),
        pl.BlockSpec((SUFFIX, 1), lambda r, s: (r, 0)),
        pl.BlockSpec((1, 1, cols), lambda r, s: (r, 0, block)),
        pl.BlockSpec((1, cols), lambda r, s: (0, block)),
        pl.BlockSpec((parts, 1, rows, cols), lambda r, s: (0, s[r], 0, block)),
    ]
    aliases = {}
    if carry:
        in_specs += [pl.BlockSpec(memory_space=pl.ANY)] * len(carry)
        aliases = {12 + i: i for i in range(len(carry))}
    flops = 2 * tokens * cols * (2 * state_size + 2 * SUFFIX)
    return pl.pallas_call(
        functools.partial(ssd_kernel, first, heads, width, len(carry)),
        out_shape=(
            jax.ShapeDtypeStruct((tokens, total_cols), jnp.bfloat16),
            jax.ShapeDtypeStruct((requests, state_size, total_cols), jnp.bfloat16),
        ),
        grid_spec=pltpu.PrefetchScalarGridSpec(
            num_scalar_prefetch=1,
            grid=(requests,),
            in_specs=in_specs,
            out_specs=(
                pl.BlockSpec((SUFFIX, cols), lambda r, s: (r, block)),
                pl.BlockSpec((1, state_size, cols), lambda r, s: (r, 0, block)),
            ),
            scratch_shapes=[pltpu.VMEM((SUFFIX, cols), jnp.bfloat16)],
        ),
        input_output_aliases=aliases,
        compiler_params=pltpu.CompilerParams(vmem_limit_bytes=48 * 1024 * 1024),
        cost_estimate=pl.CostEstimate(
            flops=flops,
            bytes_accessed=4 * cols * (tokens + requests * state_size),
            transcendentals=tokens * SUFFIX * heads,
        ),
    )(places, chan, proj_bc, cum, cum_t, step_t, factor, grown, live, keep, gain, state, *carry)


MESH = pl.DeviceIdType.MESH


def flip(index, bits):
    result = index
    for bit in (1, 2, 4):
        if bits & bit:
            result = result + bit - 2 * bit * ((index // bit) % 2)
    return result


def project(tokens_vmem, w_ref, out_ref, total, tile):
    depth, cols = w_ref.shape
    rows = tokens_vmem.shape[0]
    k_tile = min(depth, 2048)
    steps = depth // k_tile

    def step(w_block, out_block):
        k = pl.program_id(1)
        columns = pl.ds(pl.multiple_of(k * k_tile, k_tile), k_tile)
        part = jnp.dot(
            tokens_vmem[:, columns], w_block[...], preferred_element_type=jnp.float32
        )

        @pl.when(k == 0)
        def _():
            total[:, :tile] = part

        @pl.when(k > 0)
        def _():
            total[:, :tile] += part

        @pl.when(k == steps - 1)
        def _():
            out_block[...] = total[:, :tile].astype(out_block.dtype)

    pltpu.emit_pipeline(
        step,
        grid=(cols // tile, steps),
        in_specs=[pl.BlockSpec((k_tile, tile), lambda n, k: (k, n))],
        out_specs=[pl.BlockSpec((rows, tile), lambda n, k: (0, n))],
    )(w_ref, out_ref)


def exchange_kernel(bc_cols, tile, slots_ref, tokens_ref, small_ref, x_ref, pool_ref, chan_ref, proj_ref, dt_ref,
                    w_small, w_all, landed, state_ref, tokens_vmem, pool_vmem, picked, stage_x, stage_small, stage_z, total, w_send, w_recv, w_here,
                    snap_send, snap_recv, z_send, z_recv, z_here, local_sem):
    me, my_z = lax.axis_index("cache"), lax.axis_index("head")
    n_cache, n_head, width = picked.shape[0], picked.shape[1], picked.shape[3]
    depth = small_ref.shape[0]
    half = depth // 2

    pool_copy = pltpu.make_async_copy(pool_ref, pool_vmem, local_sem.at[0])
    pool_copy.start()
    barrier = pltpu.get_barrier_semaphore()
    for a in range(1, n_cache):
        pl.semaphore_signal(barrier, inc=1, device_id=(flip(me, a), my_z), device_id_type=MESH)
    for b in range(1, n_head):
        pl.semaphore_signal(barrier, inc=1, device_id=(me, flip(my_z, b)), device_id_type=MESH)
    pl.semaphore_wait(barrier, n_cache + n_head - 2)

    chunks = [(x_ref, w_all, c, tile) for c in range(0, x_ref.shape[1] - tile, tile)]
    for c in range(x_ref.shape[1] - tile, x_ref.shape[1], tile // 2):
        chunks.append((x_ref, w_all, c, tile // 2))
    chunks.insert(1, (small_ref, w_small, 0, small_ref.shape[1]))

    def remote(src, dst, sends, recvs, index, device):
        return pltpu.make_async_remote_copy(
            src_ref=src, dst_ref=dst, send_sem=sends.at[index], recv_sem=recvs.at[index],
            device_id=device, device_id_type=MESH,
        )

    def weights(i, kind):
        src, dst, first, width = chunks[i]
        to, owner, low, rows = (
            (2, 0, 0, depth), (4, 0, 0, depth), (1, 0, 0, depth),
            (4, 2, 0, half), (1, 2, 0, depth), (2, 4, half, half), (1, 4, 0, depth),
            (1, 6, 0, half), (1, 6, half, half),
        )[kind]
        columns = pl.ds(first, width)
        place = dst.at[pl.ds(pl.multiple_of(flip(me, owner) * depth, depth) + low, rows), columns]
        source = src.at[:, columns] if kind < 3 else place
        return remote(source, place, w_send, w_recv, (i, kind), (flip(me, to), my_z))

    def own_in(i):
        src, _, first, width = chunks[i]
        columns = pl.ds(first, width)
        stage = stage_small if src is small_ref else stage_x
        return pltpu.make_async_copy(src.at[:, columns], stage.at[:, columns], w_here.at[0, i])

    def own_out(i):
        src, dst, first, width = chunks[i]
        columns = pl.ds(first, width)
        stage = stage_small if src is small_ref else stage_x
        rows = pl.ds(pl.multiple_of(me * depth, depth), depth)
        return pltpu.make_async_copy(stage.at[:, columns], dst.at[rows, columns], w_here.at[1, i])

    def snapshot(a):
        peer = flip(me, a)
        return remote(picked.at[peer], landed.at[me], snap_send, snap_recv, (a - 1,), (peer, my_z))

    def along_z(a, b):
        peer = flip(me, a)
        to = flip(my_z, b)
        src = (landed if a else picked).at[peer, to]
        return remote(src, state_ref.at[my_z, peer], z_send, z_recv, (a, b - 1), (me, to))

    def stay_in(a):
        return pltpu.make_async_copy(
            landed.at[flip(me, a), my_z], stage_z.at[a - 1], z_here.at[0, a]
        )

    def stay_out(a):
        peer = flip(me, a)
        src = stage_z.at[a - 1] if a else picked.at[peer, my_z]
        return pltpu.make_async_copy(src, state_ref.at[my_z, peer], z_here.at[1, a])

    count = len(chunks)
    tokens_copy = pltpu.make_async_copy(tokens_ref, tokens_vmem, local_sem.at[1])

    def start_direct(i):
        for kind in range(3):
            weights(i, kind).start()
        own_in(i).wait()
        own_out(i).start()

    def arrive_direct(i):
        weights(i, 0).wait_recv()
        weights(i, 3).start()
        weights(i, 4).start()
        weights(i, 1).wait_recv()
        weights(i, 5).start()
        weights(i, 6).start()

    def arrive_diagonal(i):
        weights(i, 3).wait_recv()
        weights(i, 7).start()
        weights(i, 5).wait_recv()
        weights(i, 8).start()

    def arrive_rest(i):
        own_out(i).wait()
        for kind in (2, 4, 6, 7, 8):
            weights(i, kind).wait_recv()

    def multiply(i):
        if chunks[i][0] is small_ref:
            project(tokens_vmem, w_small.at[:, :bc_cols], proj_ref, total, min(tile, bc_cols))
            project(tokens_vmem, w_small.at[:, bc_cols:], dt_ref, total, LANES)
        else:
            columns = pl.ds(chunks[i][2], chunks[i][3])
            project(tokens_vmem, w_all.at[:, columns], chan_ref.at[:, columns], total, chunks[i][3])

    def pass_on(a):
        snapshot(a).wait_recv()
        for b in (2, 3, 1):
            along_z(a, b).start()
        stay_in(a).start()

    def pick(i, _):
        slot = slots_ref[i]
        for part in range(n_head):
            picked[i, part] = pool_vmem[slot, :, part * width : (part + 1) * width]
        return 0

    for i in range(count):
        own_in(i).start()
    start_direct(0)
    pool_copy.wait()
    lax.fori_loop(0, n_cache, pick, 0)
    for a in (6, 2, 4, 7, 3, 5, 1):
        snapshot(a).start()
    for b in (2, 3, 1):
        along_z(0, b).start()
    stay_out(0).start()
    tokens_copy.start()
    pass_on(1)
    pass_on(2)
    pass_on(4)
    start_direct(1)
    for a in (3, 5, 6, 7):
        pass_on(a)
    tokens_copy.wait()
    for a in range(1, n_cache):
        stay_in(a).wait()
        stay_out(a).start()
    for i in range(count + 1):
        if i < count:
            arrive_direct(i)
            if i + 2 < count:
                start_direct(i + 2)
        if i >= 1:
            if i < count:
                arrive_diagonal(i - 1)
            arrive_rest(i - 1)
            if i == count - 1:
                arrive_diagonal(i)
            multiply(i - 1)
    for a in range(n_cache):
        stay_out(a).wait()
        for b in range(1, n_head):
            along_z(a, b).wait()
    for a in range(1, n_cache):
        snapshot(a).wait_send()
    for i in range(count):
        for kind in range(9):
            weights(i, kind).wait_send()


def exchange(chosen, tokens, local_small, w_x, pool, n_cache, n_head, bc_cols):
    rows, model = tokens.shape
    _, state_rows, width = pool.shape
    width = width // n_head
    small_cols, cols = local_small.shape[1], w_x.shape[1]
    tile = 512
    count = 2 + cols // tile
    bf16 = jnp.bfloat16
    anywhere = pl.BlockSpec(memory_space=pl.ANY)
    dma = pltpu.SemaphoreType.DMA
    outs = pl.pallas_call(
        functools.partial(exchange_kernel, bc_cols, tile),
        out_shape=(
            jax.ShapeDtypeStruct((rows, cols), bf16),
            jax.ShapeDtypeStruct((rows, bc_cols), bf16),
            jax.ShapeDtypeStruct((rows, small_cols - bc_cols), jnp.float32),
            jax.ShapeDtypeStruct((model, small_cols), bf16),
            jax.ShapeDtypeStruct((model, cols), bf16),
            jax.ShapeDtypeStruct((n_cache, n_head, state_rows, width), bf16),
            jax.ShapeDtypeStruct((n_head, n_cache, state_rows, width), bf16),
        ),
        in_specs=[pl.BlockSpec(memory_space=pltpu.SMEM)] + [anywhere] * 4,
        out_specs=[anywhere] * 7,
        scratch_shapes=[
            pltpu.VMEM(tokens.shape, bf16),
            pltpu.VMEM(pool.shape, bf16),
            pltpu.VMEM((n_cache, n_head, state_rows, width), bf16),
            pltpu.VMEM(w_x.shape, bf16),
            pltpu.VMEM(local_small.shape, bf16),
            pltpu.VMEM((n_cache - 1, state_rows, width), bf16),
            pltpu.VMEM((rows, tile), jnp.float32),
            dma((count, 9)),
            dma((count, 9)),
            dma((2, count)),
            dma((n_cache - 1,)),
            dma((n_cache - 1,)),
            dma((n_cache, n_head - 1)),
            dma((n_cache, n_head - 1)),
            dma((2, n_cache)),
            dma((2,)),
        ],
        compiler_params=pltpu.CompilerParams(
            collective_id=0, has_side_effects=True, vmem_limit_bytes=56 * 1024 * 1024
        ),
        cost_estimate=pl.CostEstimate(
            flops=2 * rows * model * (cols + small_cols),
            bytes_accessed=4 * model * (cols + small_cols),
            transcendentals=0,
        ),
    )(chosen, tokens, local_small, w_x, pool)
    return outs[0], outs[1], outs[2], outs[6]


def body(tokens, w_x, w_bc, w_dt, dt_bias, decay_log, skip_gain, pool, owners, slots, offsets):
    token_count = tokens.shape[0]
    requests_here = token_count // SUFFIX
    heads_here = dt_bias.shape[0]
    groups_here = w_bc.shape[1]
    per_group = heads_here // groups_here
    total_cols = w_x.shape[1]
    head_width = total_cols // heads_here
    bc_cols = w_bc.shape[1] * w_bc.shape[2]
    cache_count = lax.axis_size("cache")
    head_count = lax.axis_size("head")
    my_cache = lax.axis_index("cache")

    one_kernel = cache_count == 8 and head_count == 4
    chunks = []
    for group in range(groups_here):
        pieces = 2 if group == groups_here - 1 and not one_kernel else 1
        size = per_group // pieces
        chunks += [(group * per_group + i * size, size, group) for i in range(pieces)]

    pad = -w_dt.shape[1] % LANES
    local_small = jnp.concatenate(
        [w_bc.reshape(w_bc.shape[0], bc_cols), jnp.pad(w_dt, ((0, 0), (0, pad)))], axis=1
    )
    owner_table = owners[:, 0].reshape(cache_count, requests_here)
    slot_table = slots[:, 0].reshape(cache_count, requests_here)
    chosen_slot = jnp.sum(jnp.where(owner_table == my_cache, slot_table, 0), axis=1)
    my_owners = lax.dynamic_slice_in_dim(owners[:, 0], my_cache * requests_here, requests_here)

    if one_kernel:
        chan_all, proj_bc, part_dt, state = exchange(
            chosen_slot, tokens, local_small, w_x, pool, cache_count, head_count, bc_cols
        )
        places = my_owners
    else:
        w_small = lax.all_gather(local_small, "cache", axis=0, tiled=True)
        w_parts = [
            lax.all_gather(
                w_x[:, first * head_width : (first + size) * head_width],
                "cache",
                axis=0,
                tiled=True,
            )
            for first, size, _ in chunks
        ]
        blocks = pick_for_owners(pool, chosen_slot, head_count)
        received = lax.all_to_all(blocks, "cache", split_axis=0, concat_axis=0, tiled=True)
        wanted = pick_for_requests(received, my_owners)
        state = lax.all_to_all(wanted, "head", split_axis=0, concat_axis=0, tiled=True)
        places = jnp.arange(requests_here, dtype=jnp.int32)
        part_small = jnp.dot(tokens, w_small, preferred_element_type=jnp.float32)
        proj_bc = part_small[:, :bc_cols].astype(jnp.bfloat16)
        part_dt = part_small[:, bc_cols:]
    dt_raw = part_dt[:, :heads_here].reshape(requests_here, SUFFIX, heads_here)
    positions = jnp.arange(SUFFIX, dtype=jnp.int32)
    live = (positions[None, :] >= offsets[:, None]).astype(jnp.float32)
    step = jax.nn.softplus(dt_raw + dt_bias[None, None, :]) * live[:, :, None]
    rate = -jnp.exp(decay_log)[None, None, :] * step
    cum = jnp.cumsum(rate, axis=1)
    last = cum[:, -1:, :]
    factor = jnp.exp(last - cum) * step
    small = (
        cum.reshape(token_count, heads_here),
        jnp.transpose(cum, (0, 2, 1)),
        jnp.transpose(step, (0, 2, 1)),
        factor.reshape(token_count, heads_here),
        jnp.exp(cum).reshape(token_count, heads_here),
        live.reshape(token_count, 1),
        jnp.repeat(jnp.exp(last), head_width, axis=2),
        jnp.repeat(skip_gain, head_width)[None, :],
    )

    carry = ()
    for place, (first, size, group) in enumerate(chunks):
        if one_kernel:
            chan = chan_all
        else:
            chan = jnp.dot(tokens, w_parts[place], preferred_element_type=jnp.float32)
            chan = chan.astype(jnp.bfloat16)
        carry = ssd(
            first, size, group, chan, proj_bc, small, state, places, carry, total_cols
        )
    return tuple(carry)


def solution(mesh):
    return jax.shard_map(
        body,
        mesh=mesh,
        in_specs=(
            P("cache", None),
            P("cache", "head"),
            P("cache", "head", None),
            P("cache", "head"),
            P("head"),
            P("head"),
            P("head"),
            P("cache", "head", None),
            P(),
            P(),
            P("cache"),
        ),
        out_specs=(P("cache", "head"), P("cache", None, "head")),
        check_vma=False,
    )
```
